32 devices in a mesh: dp: 8 (over z, x), tensor: 4 (over y, core).
Axes of the slice: x: 2, y: 2, z: 4, core: 2. Of those that a mesh axis runs over, the one named last changes fastest.
Arguments:
- tokens: bfloat16 [16384, 1024], P(('dp', 'tensor')), may hold values from -6 to 6
- mixer_gain: float32 [1024], replicated, may hold values from 0.25 to 1.75
- in_weight: bfloat16 [3, 1024, 1024], P(None, None, 'tensor'), may hold values from -0.1875 to 0.1875
- conv_weight: float32 [3, 1024], P(None, 'tensor'), may hold values from -3 to 3
- out_weight: bfloat16 [1024, 1024], P('tensor'), may hold values from -0.1875 to 0.1875
- mlp_gain: float32 [1024], replicated, may hold values from 0.25 to 1.75
- gate_weight: bfloat16 [1024, 4608], P(None, 'tensor'), may hold values from -0.1875 to 0.1875
- up_weight: bfloat16 [1024, 4608], P(None, 'tensor'), may hold values from -0.1875 to 0.1875
- down_weight: bfloat16 [4608, 1024], P('tensor'), may hold values from -0.125 to 0.125
- out_grad: bfloat16 [16384, 1024], P(('dp', 'tensor')), may hold values from -6 to 6
Outputs:
- output: bfloat16 [16384, 1024], P(('dp', 'tensor'))
- input_grad: bfloat16 [16384, 1024], P(('dp', 'tensor'))
- mixer_gain_grad: float32 [1024], replicated
- in_weight_grad: float32 [3, 1024, 1024], P(None, None, 'tensor')
- conv_weight_grad: float32 [3, 1024], P(None, 'tensor')
- out_weight_grad: float32 [1024, 1024], P('tensor')
- mlp_gain_grad: float32 [1024], replicated
- gate_weight_grad: float32 [1024, 4608], P(None, 'tensor')
- up_weight_grad: float32 [1024, 4608], P(None, 'tensor')
- down_weight_grad: float32 [4608, 1024], P('tensor')
The draws below stay inside these ranges and needn't reach their ends.
All inputs are finite; a program needn't handle non-finite values.
Results may differ from the reference program's by a relative error of at most 0.011.
Values may be sent and summed in bfloat16 or wider, within the bound.
A program may use at most 192 MiB of HBM per device.

```python
import math
import jax
import jax.numpy as jnp
from jax import lax

D = 1024
FF = 4608
LEN = 1024
TOKENS = 16384


def steps_of(rng, extent, shards, smallest, high):
    gain, own = 1.0, jax.random.fold_in(rng, 6)
    for axis_at, blocks in shards:
        heights = jnp.exp(jax.random.uniform(jax.random.fold_in(own, axis_at), (blocks,), jnp.float32, smallest / len(shards), high / len(shards)))
        gain = gain * jnp.repeat(heights, extent[axis_at] // blocks).reshape([-1 if axis == axis_at else 1 for axis in range(len(extent))])
    return gain


def centred(stream_key, shape, scale, limit, cuts=(), dtype=jnp.bfloat16):
    values = jax.random.normal(stream_key, shape, jnp.float32) * scale
    if len(cuts) > 0:
        values = steps_of(stream_key, shape, cuts, -0.22, 0.18) * values
    return jnp.clip(values, min=-limit, max=limit).astype(dtype)


def setup_inputs(seed: int = 0) -> dict:
    key_list = jax.random.split(jax.random.key(seed), 11)
    tokens = centred(key_list[0], (TOKENS, D), 1.0, 6.0, ((0, 32),))
    mixer_gain = jnp.clip(1.0 + 0.15 * jax.random.normal(key_list[1], (D,), jnp.float32), 0.25, 1.75)
    in_weight = centred(key_list[2], (3, D, D), D ** -0.5, 0.1875, ((2, 4),))
    conv_weight = centred(key_list[3], (3, D), 0.6, 3.0, ((1, 4),), jnp.float32)
    out_weight = centred(key_list[4], (D, D), D ** -0.5, 0.1875, ((0, 4),))
    mlp_gain = jnp.clip(1.0 + 0.15 * jax.random.normal(key_list[5], (D,), jnp.float32), 0.25, 1.75)
    gate_weight = centred(key_list[6], (D, FF), D ** -0.5, 0.1875, ((1, 4),))
    up_weight = centred(key_list[7], (D, FF), D ** -0.5, 0.1875, ((1, 4),))
    down_weight = centred(key_list[8], (FF, D), (FF // 2) ** -0.5, 0.125, ((0, 4),))
    out_grad = centred(key_list[9], (TOKENS, D), 1.0, 6.0, ((0, 32),))
    return dict(tokens=tokens, mixer_gain=mixer_gain, in_weight=in_weight, conv_weight=conv_weight, out_weight=out_weight, mlp_gain=mlp_gain, gate_weight=gate_weight, up_weight=up_weight, down_weight=down_weight, out_grad=out_grad)


@jax.custom_vjp
def low(v):
    return lax.optimization_barrier(v.astype(jnp.bfloat16)).astype(jnp.float32)

@jax.custom_vjp
def low_back(v):
    return v

def low_keep(v):
    return (low(v), None)

def low_pass(kept, grad):
    return (grad,)

def back_keep(v):
    return (v, None)

def back_low(kept, grad):
    return (low(grad),)
low.defvjp(low_keep, low_pass)
low_back.defvjp(back_keep, back_low)
HIGH = lax.Precision.HIGHEST

def rms_scale(values):
    return lax.rsqrt(lax.optimization_barrier(jnp.mean(values * values, axis=-1, keepdims=True)) + 1e-05)

def forward(inputs, mixer_gain, in_weight, conv_weight, out_weight, mlp_gain, gate_weight, up_weight, down_weight):
    first = low(inputs * rms_scale(inputs) * mixer_gain)
    streams = low_back(jnp.einsum('td,kdc->ktc', first, in_weight, precision=HIGH))
    product = (streams[0] * streams[2]).reshape(-1, LEN, inputs.shape[1])
    padded = jnp.pad(product, ((0, 0), (2, 0), (0, 0)))
    mixed = conv_weight[0] * padded[:, :-2] + conv_weight[1] * padded[:, 1:-1] + conv_weight[2] * padded[:, 2:]
    gated = low(streams[1] * mixed.reshape(-1, inputs.shape[1]))
    middle = inputs + low_back(jnp.dot(gated, out_weight, precision=HIGH))
    second = low(middle * rms_scale(middle) * mlp_gain)
    gate = low_back(jnp.dot(second, gate_weight, precision=HIGH))
    upper = low_back(jnp.dot(second, up_weight, precision=HIGH))
    hidden = low(jax.nn.silu(gate) * upper)
    return middle + jnp.dot(hidden, down_weight, precision=HIGH)

def reference(tokens, mixer_gain, in_weight, conv_weight, out_weight, mlp_gain, gate_weight, up_weight, down_weight, out_grad):
    width = tokens.shape[1]
    num_seqs = tokens.shape[0] // LEN
    group = math.gcd(num_seqs, 4)
    blocks = num_seqs // group
    params = tuple((w.astype(jnp.float32) for w in (mixer_gain, in_weight, conv_weight, out_weight, mlp_gain, gate_weight, up_weight, down_weight)))
    rows_in = tokens.astype(jnp.float32).reshape(blocks, group * LEN, width)
    rows_grad = out_grad.astype(jnp.float32).reshape(blocks, group * LEN, width)

    def one_block(carry, block):
        inputs, cotangent = block
        result, pull = jax.vjp(forward, inputs, *params)
        grads = pull(cotangent)
        updated = tuple((total + part for total, part in zip(carry, grads[1:])))
        return (updated, (result, grads[0]))
    start = tuple((jnp.zeros_like(w) for w in params))
    totals, (results, input_grads) = lax.scan(one_block, start, (rows_in, rows_grad))
    output = results.reshape(-1, width).astype(jnp.bfloat16)
    input_grad = input_grads.reshape(-1, width).astype(jnp.bfloat16)
    return (output, input_grad, totals[0], totals[1], totals[2], totals[3], totals[4], totals[5], totals[6], totals[7])
```

```python
import functools

import jax
import jax.numpy as jnp
from jax import lax
from jax.sharding import PartitionSpec as P

LEN = 1024
F32 = jnp.float32
BF16 = jnp.bfloat16


def rms_scale(values):
    return lax.rsqrt(jnp.mean(values * values, axis=-1, keepdims=True) + 1e-05)


def norm_back(upstream, values, scale, gain_vec):
    scaled = upstream * gain_vec
    inner = jnp.mean(scaled * values, axis=-1, keepdims=True)
    return scale * (scaled - values * scale * scale * inner)


def dot(a, b):
    return jnp.dot(a, b, preferred_element_type=F32)


def dot_rows(a, b):
    return lax.dot_general(a, b, (((0,), (0,)), ((), ())), preferred_element_type=F32)


def dot_cols(a, b):
    return lax.dot_general(a, b, (((1,), (1,)), ((), ())), preferred_element_type=F32)


def body(
    size,
    tokens,
    mixer_gain,
    in_weight,
    conv_weight,
    out_weight,
    mlp_gain,
    gate_weight,
    up_weight,
    down_weight,
    out_grad,
):
    n_dp, n_tensor = size["dp"], size["tensor"]
    chans = in_weight.shape[2]
    dp_at = lax.axis_index("dp")
    core = lax.rem(lax.axis_index("tensor"), 2)

    def swap(value, axis, bit):
        return lax.ppermute(value, axis, [(i, i ^ bit) for i in range(size[axis])])

    def ordered(side, own, other):
        return jnp.where(side == 0, jnp.concatenate([own, other]), jnp.concatenate([other, own]))

    def parted(side, value):
        two = value.reshape(2, value.shape[0] // 2, *value.shape[1:])
        keep = lax.dynamic_index_in_dim(two, side, 0, keepdims=False)
        give = lax.dynamic_index_in_dim(two, 1 - side, 0, keepdims=False)
        return keep, give

    def gather(own):
        far = swap(own, "tensor", 2)
        near = swap(own, "tensor", 1)
        far_near = swap(far, "tensor", 1)
        return ordered(core, own, near), ordered(core, far, far_near)

    def scatter(mine, other):
        keep, give = parted(core, other)
        total = keep + swap(give.astype(BF16), "tensor", 1).astype(F32)
        got_far = swap(total.astype(BF16), "tensor", 2)
        keep, give = parted(core, mine)
        return keep + swap(give.astype(BF16), "tensor", 1).astype(F32) + got_far.astype(F32)

    dp_bits = [1 << k for k in range(n_dp.bit_length() - 1)]

    def sum_dp(value, turn):
        bits = dp_bits[turn:] + dp_bits[:turn]
        current = value
        for bit in bits:
            keep, give = parted((dp_at // bit) % 2, current)
            current = keep + swap(give.astype(BF16), "dp", bit).astype(F32)
        current = current.astype(BF16)
        for bit in reversed(bits):
            current = ordered((dp_at // bit) % 2, current, swap(current, "dp", bit))
        return current.astype(F32)

    def sum_dp_split(value):
        half = value.shape[0] // 2
        return jnp.concatenate([sum_dp(value[:half], 0), sum_dp(value[half:], 1)])

    def sum_small(value, axis):
        bit = 1
        while bit < size[axis]:
            value = value + swap(value, axis, bit)
            bit *= 2
        return value

    in_flat = jnp.concatenate([in_weight[0], in_weight[1], in_weight[2]], axis=1)

    def conv_forward(first):
        streams = dot(first, in_flat)
        b, c, x = streams[:, :chans], streams[:, chans : 2 * chans], streams[:, 2 * chans :]
        product = (b * x).reshape(-1, LEN, chans)
        padded = jnp.pad(product, ((0, 0), (2, 0), (0, 0)))
        mixed = (
            conv_weight[0] * padded[:, :-2]
            + conv_weight[1] * padded[:, 1:-1]
            + conv_weight[2] * padded[:, 2:]
        ).reshape(-1, chans)
        gated = (c * mixed).astype(BF16)
        return (b, c, x, padded, mixed, gated), dot(gated, out_weight)

    def conv_backward(kept, branch_grad):
        b, c, x, padded, mixed, gated = kept
        gated_grad = dot_cols(branch_grad, out_weight)
        mixed_grad = (gated_grad * c).reshape(-1, LEN, chans)
        c_grad = gated_grad * mixed
        trailing = jnp.pad(mixed_grad, ((0, 0), (0, 2), (0, 0)))
        product_grad = (
            conv_weight[2] * trailing[:, :-2]
            + conv_weight[1] * trailing[:, 1:-1]
            + conv_weight[0] * trailing[:, 2:]
        ).reshape(-1, chans)
        conv_grad = jnp.stack(
            [jnp.sum(mixed_grad * padded[:, tap : tap + LEN], axis=(0, 1)) for tap in range(3)]
        )
        stream_grad = jnp.concatenate(
            [product_grad * x, c_grad, product_grad * b], axis=1
        ).astype(BF16)
        return stream_grad, conv_grad, dot_cols(stream_grad, in_flat)

    def mlp_forward(second):
        gate = dot(second, gate_weight)
        upper = dot(second, up_weight)
        hidden = (gate * jax.nn.sigmoid(gate) * upper).astype(BF16)
        return gate, upper, hidden

    def mlp_backward(gate, upper, cotangent):
        hidden_grad = dot_cols(cotangent, down_weight)
        sigma = jax.nn.sigmoid(gate)
        gate_grad = (hidden_grad * upper * sigma * (1.0 + gate * (1.0 - sigma))).astype(BF16)
        up_grad = (hidden_grad * gate * sigma).astype(BF16)
        return gate_grad, up_grad, dot_cols(gate_grad, gate_weight) + dot_cols(up_grad, up_weight)

    inputs = tokens.astype(F32)
    scale_one = rms_scale(inputs)
    first_m, first_o = gather((inputs * scale_one * mixer_gain).astype(BF16))
    kept_o, part_o = conv_forward(first_o)
    kept_m, part_m = conv_forward(first_m)
    middle = inputs + scatter(part_m, part_o)
    scale_two = rms_scale(middle)
    second_m, second_o = gather((middle * scale_two * mlp_gain).astype(BF16))
    cot_m, cot_o = gather(out_grad)
    gate_m, upper_m, hidden_m = mlp_forward(second_m)
    gate_o, upper_o, hidden_o = mlp_forward(second_o)
    down_grad = sum_dp_split(dot_rows(hidden_m, cot_m) + dot_rows(hidden_o, cot_o))
    output = (middle + scatter(dot(hidden_m, down_weight), dot(hidden_o, down_weight))).astype(BF16)

    gate_grad_o, up_grad_o, back_o = mlp_backward(gate_o, upper_o, cot_o)
    gate_grad_m, up_grad_m, back_m = mlp_backward(gate_m, upper_m, cot_m)
    second_grad = scatter(back_m, back_o)
    gate_w_grad = sum_dp_split(dot_rows(second_m, gate_grad_m) + dot_rows(second_o, gate_grad_o))
    up_w_grad = sum_dp_split(dot_rows(second_m, up_grad_m) + dot_rows(second_o, up_grad_o))

    mlp_gain_part = jnp.sum(second_grad * middle * scale_two, axis=0)
    middle_grad = out_grad.astype(F32) + norm_back(second_grad, middle, scale_two, mlp_gain)
    branch_m, branch_o = gather(middle_grad.astype(BF16))
    out_w_grad = sum_dp(dot_rows(kept_m[5], branch_m) + dot_rows(kept_o[5], branch_o), 1)
    stream_grad_o, conv_grad_o, back_o = conv_backward(kept_o, branch_o)
    stream_grad_m, conv_grad_m, back_m = conv_backward(kept_m, branch_m)
    in_flat_grad = dot_rows(first_m, stream_grad_m) + dot_rows(first_o, stream_grad_o)
    in_w_grad = jnp.stack(
        [sum_dp(in_flat_grad[:, k * chans : (k + 1) * chans], k % 2) for k in range(3)]
    )
    first_grad = scatter(back_m, back_o)
    mixer_gain_part = jnp.sum(first_grad * inputs * scale_one, axis=0)
    input_grad = (middle_grad + norm_back(first_grad, inputs, scale_one, mixer_gain)).astype(BF16)

    conv_grad = sum_small(conv_grad_m + conv_grad_o, "dp")
    gains = sum_small(sum_small(jnp.stack([mixer_gain_part, mlp_gain_part]), "tensor"), "dp")
    return (
        output,
        input_grad,
        gains[0],
        in_w_grad,
        conv_grad,
        out_w_grad,
        gains[1],
        gate_w_grad,
        up_w_grad,
        down_grad,
    )


def solution(mesh):
    size = {"dp": mesh.shape["dp"], "tensor": mesh.shape["tensor"]}
    return jax.shard_map(
        functools.partial(body, size),
        mesh=mesh,
        in_specs=(
            P(("dp", "tensor"), None),
            P(),
            P(None, None, "tensor"),
            P(None, "tensor"),
            P("tensor", None),
            P(),
            P(None, "tensor"),
            P(None, "tensor"),
            P("tensor", None),
            P(("dp", "tensor"), None),
        ),
        out_specs=(
            P(("dp", "tensor"), None),
            P(("dp", "tensor"), None),
            P(),
            P(None, None, "tensor"),
            P(None, "tensor"),
            P("tensor", None),
            P(),
            P(None, "tensor"),
            P(None, "tensor"),
            P("tensor", None),
        ),
        check_vma=False,
    )
```

```python
import functools

import jax
import jax.numpy as jnp
from jax import lax
from jax.experimental import pallas as pl
from jax.experimental.pallas import tpu as pltpu
from jax.sharding import PartitionSpec as P

LEN = 1024
ROWS = 512
F32 = jnp.float32
BF16 = jnp.bfloat16


def rms_scale(values):
    return lax.rsqrt(jnp.mean(values * values, axis=-1, keepdims=True) + 1e-05)


def norm_back(upstream, values, scale, gain_vec):
    scaled = upstream * gain_vec
    inner = jnp.mean(scaled * values, axis=-1, keepdims=True)
    return scale * (scaled - values * scale * scale * inner)


def dot(a, b):
    return jnp.dot(a, b, preferred_element_type=F32)


def dot_rows(a, b):
    return lax.dot_general(a, b, (((0,), (0,)), ((), ())), preferred_element_type=F32)


def dot_cols(a, b):
    return lax.dot_general(a, b, (((1,), (1,)), ((), ())), preferred_element_type=F32)


def after(value, *others):
    return lax.optimization_barrier((value, *others))[0]


def mlp_kernel(
    second_ref,
    cot_ref,
    gate_ref,
    up_ref,
    down_ref,
    out_ref,
    back_ref,
    gate_grad_ref,
    up_grad_ref,
    down_grad_ref,
    gate_sum,
    up_sum,
    down_sum,
):
    step = pl.program_id(0)
    second, cot = second_ref[...], cot_ref[...]
    gate = dot(second, gate_ref[...])
    upper = dot(second, up_ref[...])
    sigma = jax.nn.sigmoid(gate)
    active = gate * sigma
    hidden = (active * upper).astype(BF16)
    out_ref[...] = dot(hidden, down_ref[...]).astype(BF16)
    hidden_grad = dot_cols(cot, down_ref[...])
    gate_grad = (hidden_grad * upper * sigma * (1.0 + gate * (1.0 - sigma))).astype(BF16)
    up_grad = (hidden_grad * active).astype(BF16)
    back_ref[...] = (dot_cols(gate_grad, gate_ref[...]) + dot_cols(up_grad, up_ref[...])).astype(BF16)
    parts = (
        (gate_sum, dot_rows(second, gate_grad)),
        (up_sum, dot_rows(second, up_grad)),
        (down_sum, dot_rows(hidden, cot)),
    )

    @pl.when(step == 0)
    def _():
        for total, part in parts:
            total[...] = part

    @pl.when(step > 0)
    def _():
        for total, part in parts:
            total[...] += part

    @pl.when(step == pl.num_programs(0) - 1)
    def _():
        gate_grad_ref[...] = gate_sum[...].astype(BF16)
        up_grad_ref[...] = up_sum[...].astype(BF16)
        down_grad_ref[...] = down_sum[...].astype(BF16)


def mlp(second, cot, gate_weight, up_weight, down_weight):
    rows, width = second.shape
    units = gate_weight.shape[1]
    tile = min(ROWS, rows)
    by_rows = pl.BlockSpec((tile, width), lambda i: (i, 0))

    def whole(shape):
        return pl.BlockSpec(shape, lambda i: (0, 0), pipeline_mode=pl.Buffered(1))

    wide, tall = (width, units), (units, width)
    return pl.pallas_call(
        mlp_kernel,
        grid=(rows // tile,),
        in_specs=[by_rows, by_rows, whole(wide), whole(wide), whole(tall)],
        out_specs=[by_rows, by_rows, whole(wide), whole(wide), whole(tall)],
        out_shape=[jax.ShapeDtypeStruct((rows, width), BF16)] * 2
        + [jax.ShapeDtypeStruct(wide, BF16)] * 2
        + [jax.ShapeDtypeStruct(tall, BF16)],
        scratch_shapes=[pltpu.VMEM(wide, F32), pltpu.VMEM(wide, F32), pltpu.VMEM(tall, F32)],
        compiler_params=pltpu.CompilerParams(vmem_limit_bytes=56 << 20),
        cost_estimate=pl.CostEstimate(
            flops=18 * rows * width * units,
            bytes_accessed=12 * width * units + 8 * rows * width,
            transcendentals=rows * units,
        ),
    )(second, cot, gate_weight, up_weight, down_weight)


def body(
    size,
    tokens,
    mixer_gain,
    in_weight,
    conv_weight,
    out_weight,
    mlp_gain,
    gate_weight,
    up_weight,
    down_weight,
    out_grad,
):
    n_dp, n_tensor = size["dp"], size["tensor"]
    chans = in_weight.shape[2]
    dp_at = lax.axis_index("dp")
    core = lax.rem(lax.axis_index("tensor"), 2)

    def swap(value, axis, bit):
        return lax.ppermute(value, axis, [(i, i ^ bit) for i in range(size[axis])])

    def ordered(side, own, other):
        return jnp.where(side == 0, jnp.concatenate([own, other]), jnp.concatenate([other, own]))

    def parted(side, value):
        two = value.reshape(2, value.shape[0] // 2, *value.shape[1:])
        keep = lax.dynamic_index_in_dim(two, side, 0, keepdims=False)
        give = lax.dynamic_index_in_dim(two, 1 - side, 0, keepdims=False)
        return keep, give

    def gather(own):
        far = swap(own, "tensor", 2)
        near = swap(own, "tensor", 1)
        far_near = swap(far, "tensor", 1)
        return ordered(core, own, near), ordered(core, far, far_near)

    def scatter(mine, other):
        keep, give = parted(core, other)
        total = keep.astype(F32) + swap(give.astype(BF16), "tensor", 1).astype(F32)
        total = total.astype(BF16)
        got_far = swap(total, "tensor", 2)
        keep, give = parted(core, mine)
        near = keep.astype(F32) + swap(give.astype(BF16), "tensor", 1).astype(F32)
        return near + got_far.astype(F32), total

    dp_bits = [1 << k for k in range(n_dp.bit_length() - 1)]

    def order_of(turn):
        return dp_bits[turn:] + dp_bits[:turn]

    def reduce_dp(value, turn=0):
        current = value
        for bit in order_of(turn):
            keep, give = parted((dp_at // bit) % 2, current)
            current = keep + swap(give.astype(BF16), "dp", bit).astype(F32)
        return current.astype(BF16)

    def spread_dp(current, turn=0):
        for bit in reversed(order_of(turn)):
            current = ordered((dp_at // bit) % 2, current, swap(current, "dp", bit))
        return current.astype(F32)

    def sum_dp(value, turn=0):
        return spread_dp(reduce_dp(value, turn), turn)

    def sum_small(value, axis):
        bit = 1
        while bit < size[axis]:
            value = value + swap(value, axis, bit)
            bit *= 2
        return value

    in_flat = jnp.concatenate([in_weight[0], in_weight[1], in_weight[2]], axis=1)

    def conv_forward(first):
        streams = dot(first, in_flat)
        b, c, x = streams[:, :chans], streams[:, chans : 2 * chans], streams[:, 2 * chans :]
        product = (b * x).reshape(-1, LEN, chans)
        padded = jnp.pad(product, ((0, 0), (2, 0), (0, 0)))
        mixed = (
            conv_weight[0] * padded[:, :-2]
            + conv_weight[1] * padded[:, 1:-1]
            + conv_weight[2] * padded[:, 2:]
        ).reshape(-1, chans)
        gated = (c * mixed).astype(BF16)
        return (b, c, x, padded, mixed, gated), dot(gated, out_weight)

    def conv_backward(kept, branch_grad):
        b, c, x, padded, mixed, gated = kept
        gated_grad = dot_cols(branch_grad, out_weight)
        mixed_grad = (gated_grad * c).reshape(-1, LEN, chans)
        c_grad = gated_grad * mixed
        trailing = jnp.pad(mixed_grad, ((0, 0), (0, 2), (0, 0)))
        product_grad = (
            conv_weight[2] * trailing[:, :-2]
            + conv_weight[1] * trailing[:, 1:-1]
            + conv_weight[0] * trailing[:, 2:]
        ).reshape(-1, chans)
        conv_grad = jnp.stack(
            [jnp.sum(mixed_grad * padded[:, tap : tap + LEN], axis=(0, 1)) for tap in range(3)]
        )
        stream_grad = jnp.concatenate(
            [product_grad * x, c_grad, product_grad * b], axis=1
        ).astype(BF16)
        return stream_grad, conv_grad, dot_cols(stream_grad, in_flat)

    inputs = tokens.astype(F32)
    scale_one = rms_scale(inputs)
    first_m, first_o = gather((inputs * scale_one * mixer_gain).astype(BF16))
    cot_m, cot_o = gather(after(out_grad, first_o))
    kept_o, part_o = conv_forward(first_o)
    kept_m, part_m = conv_forward(first_m)
    middle = inputs + scatter(part_m, part_o)[0]
    scale_two = rms_scale(middle)
    second_m, second_o = gather((middle * scale_two * mlp_gain).astype(BF16))
    out_m, back_m, *w_grads_m = mlp(second_m, cot_m, gate_weight, up_weight, down_weight)
    out_o, back_o, *w_grads_o = mlp(second_o, cot_o, gate_weight, up_weight, down_weight)
    second_grad, sent = scatter(back_m, back_o)

    halves = []
    for grad_m, grad_o in zip(w_grads_m, w_grads_o):
        half = grad_m.shape[0] // 2
        for rows in (slice(0, half), slice(half, None)):
            halves.append(grad_m[rows].astype(F32) + grad_o[rows].astype(F32))
    pieces = [reduce_dp(half) for half in halves[:2]]
    pieces += [reduce_dp(after(half, sent)) for half in halves[2:4]]

    mlp_gain_part = jnp.sum(second_grad * middle * scale_two, axis=0)
    middle_grad = out_grad.astype(F32) + norm_back(second_grad, middle, scale_two, mlp_gain)
    branch_m, branch_o = gather(middle_grad.astype(BF16))
    pieces += [reduce_dp(after(half, branch_o)) for half in halves[4:]]
    sums = [spread_dp(after(piece, branch_o)) for piece in pieces]
    gate_w_grad, up_w_grad, down_grad = (
        jnp.concatenate(sums[k : k + 2]) for k in range(0, 6, 2)
    )
    output = (middle + scatter(after(out_m, branch_o), after(out_o, branch_o))[0]).astype(BF16)

    out_w_grad = sum_dp(dot_rows(kept_m[5], branch_m) + dot_rows(kept_o[5], branch_o), 1)
    stream_grad_o, conv_grad_o, back_o = conv_backward(kept_o, branch_o)
    stream_grad_m, conv_grad_m, back_m = conv_backward(kept_m, branch_m)
    in_flat_grad = dot_rows(first_m, stream_grad_m) + dot_rows(first_o, stream_grad_o)
    in_w_grad = jnp.stack(
        [sum_dp(in_flat_grad[:, k * chans : (k + 1) * chans], k % 2) for k in range(3)]
    )
    first_grad = scatter(back_m, back_o)[0]
    mixer_gain_part = jnp.sum(first_grad * inputs * scale_one, axis=0)
    input_grad = (middle_grad + norm_back(first_grad, inputs, scale_one, mixer_gain)).astype(BF16)

    conv_grad = sum_small(conv_grad_m + conv_grad_o, "dp")
    gains = sum_small(sum_small(jnp.stack([mixer_gain_part, mlp_gain_part]), "tensor"), "dp")
    return (
        output,
        input_grad,
        gains[0],
        in_w_grad,
        conv_grad,
        out_w_grad,
        gains[1],
        gate_w_grad,
        up_w_grad,
        down_grad,
    )


def solution(mesh):
    size = {"dp": mesh.shape["dp"], "tensor": mesh.shape["tensor"]}
    return jax.shard_map(
        functools.partial(body, size),
        mesh=mesh,
        in_specs=(
            P(("dp", "tensor"), None),
            P(),
            P(None, None, "tensor"),
            P(None, "tensor"),
            P("tensor", None),
            P(),
            P(None, "tensor"),
            P(None, "tensor"),
            P("tensor", None),
            P(("dp", "tensor"), None),
        ),
        out_specs=(
            P(("dp", "tensor"), None),
            P(("dp", "tensor"), None),
            P(),
            P(None, None, "tensor"),
            P(None, "tensor"),
            P("tensor", None),
            P(),
            P(None, "tensor"),
            P(None, "tensor"),
            P("tensor", None),
        ),
        check_vma=False,
    )
```

```python
import functools

import jax
import jax.numpy as jnp
from jax import lax
from jax.experimental import pallas as pl
from jax.experimental.pallas import tpu as pltpu
from jax.sharding import PartitionSpec as P

LEN = 1024
ROWS = 512
F32 = jnp.float32
BF16 = jnp.bfloat16


def rms_scale(values):
    return lax.rsqrt(jnp.mean(values * values, axis=-1, keepdims=True) + 1e-05)


def norm_back(upstream, values, scale, gain_vec):
    scaled = upstream * gain_vec
    inner = jnp.mean(scaled * values, axis=-1, keepdims=True)
    return scale * (scaled - values * scale * scale * inner)


def dot(a, b):
    return jnp.dot(a, b, preferred_element_type=F32)


def dot_rows(a, b):
    return lax.dot_general(a, b, (((0,), (0,)), ((), ())), preferred_element_type=F32)


def dot_cols(a, b):
    return lax.dot_general(a, b, (((1,), (1,)), ((), ())), preferred_element_type=F32)


def after(value, *others):
    return lax.optimization_barrier((value, *others))[0]


def mlp_kernel(
    second_ref,
    cot_ref,
    gate_ref,
    up_ref,
    down_ref,
    out_ref,
    back_ref,
    gate_grad_ref,
    up_grad_ref,
    down_grad_ref,
    gate_sum,
    up_sum,
    down_sum,
):
    step = pl.program_id(0)
    second, cot = second_ref[...], cot_ref[...]
    gate = dot(second, gate_ref[...])
    upper = dot(second, up_ref[...])
    sigma = jax.nn.sigmoid(gate)
    active = gate * sigma
    hidden = (active * upper).astype(BF16)
    out_ref[...] = dot(hidden, down_ref[...]).astype(BF16)
    hidden_grad = dot_cols(cot, down_ref[...])
    gate_grad = (hidden_grad * upper * sigma * (1.0 + gate * (1.0 - sigma))).astype(BF16)
    up_grad = (hidden_grad * active).astype(BF16)
    back_ref[...] = (dot_cols(gate_grad, gate_ref[...]) + dot_cols(up_grad, up_ref[...])).astype(BF16)
    parts = (
        (gate_sum, dot_rows(second, gate_grad)),
        (up_sum, dot_rows(second, up_grad)),
        (down_sum, dot_rows(hidden, cot)),
    )

    @pl.when(step == 0)
    def _():
        for total, part in parts:
            total[...] = part

    @pl.when(step > 0)
    def _():
        for total, part in parts:
            total[...] += part

    @pl.when(step == pl.num_programs(0) - 1)
    def _():
        gate_grad_ref[...] = gate_sum[...].astype(BF16)
        up_grad_ref[...] = up_sum[...].astype(BF16)
        down_grad_ref[...] = down_sum[...].astype(BF16)


def mlp(second, cot, gate_weight, up_weight, down_weight):
    rows, width = second.shape
    units = gate_weight.shape[1]
    tile = min(ROWS, rows)
    by_rows = pl.BlockSpec((tile, width), lambda i: (i, 0))

    def whole(shape):
        return pl.BlockSpec(shape, lambda i: (0, 0), pipeline_mode=pl.Buffered(1))

    wide, tall = (width, units), (units, width)
    return pl.pallas_call(
        mlp_kernel,
        grid=(rows // tile,),
        in_specs=[by_rows, by_rows, whole(wide), whole(wide), whole(tall)],
        out_specs=[by_rows, by_rows, whole(wide), whole(wide), whole(tall)],
        out_shape=[jax.ShapeDtypeStruct((rows, width), BF16)] * 2
        + [jax.ShapeDtypeStruct(wide, BF16)] * 2
        + [jax.ShapeDtypeStruct(tall, BF16)],
        scratch_shapes=[pltpu.VMEM(wide, F32), pltpu.VMEM(wide, F32), pltpu.VMEM(tall, F32)],
        compiler_params=pltpu.CompilerParams(vmem_limit_bytes=56 << 20),
        cost_estimate=pl.CostEstimate(
            flops=18 * rows * width * units,
            bytes_accessed=12 * width * units + 8 * rows * width,
            transcendentals=rows * units,
        ),
    )(second, cot, gate_weight, up_weight, down_weight)


def body(
    size,
    tokens,
    mixer_gain,
    in_weight,
    conv_weight,
    out_weight,
    mlp_gain,
    gate_weight,
    up_weight,
    down_weight,
    out_grad,
):
    n_dp, n_tensor = size["dp"], size["tensor"]
    chans = in_weight.shape[2]
    dp_at = lax.axis_index("dp")
    core = lax.rem(lax.axis_index("tensor"), 2)

    def swap(value, axis, bit):
        return lax.ppermute(value, axis, [(i, i ^ bit) for i in range(size[axis])])

    def ordered(side, own, other):
        return jnp.where(side == 0, jnp.concatenate([own, other]), jnp.concatenate([other, own]))

    def parted(side, value):
        two = value.reshape(2, value.shape[0] // 2, *value.shape[1:])
        keep = lax.dynamic_index_in_dim(two, side, 0, keepdims=False)
        give = lax.dynamic_index_in_dim(two, 1 - side, 0, keepdims=False)
        return keep, give

    def gather_start(own):
        far = swap(own, "tensor", 2)
        near = swap(own, "tensor", 1)
        return ordered(core, own, near), far

    def gather_end(far):
        return ordered(core, far, swap(far, "tensor", 1))

    def gather(own):
        mine, far = gather_start(own)
        return mine, gather_end(far)

    def scatter(mine, other):
        keep, give = parted(core, other)
        total = keep.astype(F32) + swap(give.astype(BF16), "tensor", 1).astype(F32)
        total = total.astype(BF16)
        got_far = swap(total, "tensor", 2)
        keep, give = parted(core, mine)
        near = keep.astype(F32) + swap(give.astype(BF16), "tensor", 1).astype(F32)
        return near + got_far.astype(F32), total

    dp_bits = [1 << k for k in range(n_dp.bit_length() - 1)]

    def order_of(turn):
        return dp_bits[turn:] + dp_bits[:turn]

    def reduce_dp(value, turn=0):
        current = value
        for bit in order_of(turn):
            keep, give = parted((dp_at // bit) % 2, current)
            current = keep + swap(give.astype(BF16), "dp", bit).astype(F32)
        return current.astype(BF16)

    def spread_dp(current, turn=0):
        for bit in reversed(order_of(turn)):
            current = ordered((dp_at // bit) % 2, current, swap(current, "dp", bit))
        return current.astype(F32)

    def sum_dp(value, turn=0):
        return spread_dp(reduce_dp(value, turn), turn)

    def sum_small(value, axis):
        bit = 1
        while bit < size[axis]:
            value = value + swap(value, axis, bit)
            bit *= 2
        return value

    in_flat = jnp.concatenate([in_weight[0], in_weight[1], in_weight[2]], axis=1)

    def conv_forward(first):
        streams = dot(first, in_flat)
        b, c, x = streams[:, :chans], streams[:, chans : 2 * chans], streams[:, 2 * chans :]
        product = (b * x).reshape(-1, LEN, chans)
        padded = jnp.pad(product, ((0, 0), (2, 0), (0, 0)))
        mixed = (
            conv_weight[0] * padded[:, :-2]
            + conv_weight[1] * padded[:, 1:-1]
            + conv_weight[2] * padded[:, 2:]
        ).reshape(-1, chans)
        gated = (c * mixed).astype(BF16)
        return (b, c, x, padded, mixed, gated), dot(gated, out_weight)

    def conv_backward(kept, branch_grad):
        b, c, x, padded, mixed, gated = kept
        gated_grad = dot_cols(branch_grad, out_weight)
        mixed_grad = (gated_grad * c).reshape(-1, LEN, chans)
        c_grad = gated_grad * mixed
        trailing = jnp.pad(mixed_grad, ((0, 0), (0, 2), (0, 0)))
        product_grad = (
            conv_weight[2] * trailing[:, :-2]
            + conv_weight[1] * trailing[:, 1:-1]
            + conv_weight[0] * trailing[:, 2:]
        ).reshape(-1, chans)
        conv_grad = jnp.stack(
            [jnp.sum(mixed_grad * padded[:, tap : tap + LEN], axis=(0, 1)) for tap in range(3)]
        )
        stream_grad = jnp.concatenate(
            [product_grad * x, c_grad, product_grad * b], axis=1
        ).astype(BF16)
        return stream_grad, conv_grad, dot_cols(stream_grad, in_flat)

    inputs = tokens.astype(F32)
    scale_one = rms_scale(inputs)
    first_m, first_o = gather((inputs * scale_one * mixer_gain).astype(BF16))
    kept_o, part_o = conv_forward(first_o)
    kept_m, part_m = conv_forward(first_m)
    middle = inputs + scatter(part_m, part_o)[0]
    scale_two = rms_scale(middle)
    second_local = (middle * scale_two * mlp_gain).astype(BF16)
    second_m, second_far = gather_start(second_local)
    cot_m, cot_far = gather_start(after(out_grad, second_local))
    out_m, back_m, *w_grads_m = mlp(second_m, cot_m, gate_weight, up_weight, down_weight)
    second_far, cot_far, out_m = lax.optimization_barrier((second_far, cot_far, out_m))
    second_o, cot_o = gather_end(second_far), gather_end(cot_far)
    out_o, back_o, *w_grads_o = mlp(second_o, cot_o, gate_weight, up_weight, down_weight)
    second_grad, sent = scatter(back_m, back_o)

    gate_w, up_w, down_w = (m.astype(F32) + o.astype(F32) for m, o in zip(w_grads_m, w_grads_o))
    gate_piece = reduce_dp(after(gate_w, sent), 0)
    up_piece = reduce_dp(after(up_w, sent), 1)

    mlp_gain_part = jnp.sum(second_grad * middle * scale_two, axis=0)
    middle_grad = out_grad.astype(F32) + norm_back(second_grad, middle, scale_two, mlp_gain)
    branch_m, branch_o = gather(middle_grad.astype(BF16))
    down_grad = sum_dp(after(down_w, branch_o), 0)
    gate_w_grad = spread_dp(after(gate_piece, branch_o), 0)
    up_w_grad = spread_dp(after(up_piece, branch_o), 1)
    output = (middle + scatter(after(out_m, branch_o), after(out_o, branch_o))[0]).astype(BF16)

    out_w_grad = sum_dp(dot_rows(kept_m[5], branch_m) + dot_rows(kept_o[5], branch_o), 1)
    stream_grad_o, conv_grad_o, back_o = conv_backward(kept_o, branch_o)
    stream_grad_m, conv_grad_m, back_m = conv_backward(kept_m, branch_m)
    in_flat_grad = dot_rows(first_m, stream_grad_m) + dot_rows(first_o, stream_grad_o)
    in_flat_grad = sum_dp(in_flat_grad, 0)
    in_w_grad = jnp.stack([in_flat_grad[:, k * chans : (k + 1) * chans] for k in range(3)])
    first_grad = scatter(back_m, back_o)[0]
    mixer_gain_part = jnp.sum(first_grad * inputs * scale_one, axis=0)
    input_grad = (middle_grad + norm_back(first_grad, inputs, scale_one, mixer_gain)).astype(BF16)

    conv_grad = sum_small(conv_grad_m + conv_grad_o, "dp")
    gains = sum_small(sum_small(jnp.stack([mixer_gain_part, mlp_gain_part]), "tensor"), "dp")
    return (
        output,
        input_grad,
        gains[0],
        in_w_grad,
        conv_grad,
        out_w_grad,
        gains[1],
        gate_w_grad,
        up_w_grad,
        down_grad,
    )


def solution(mesh):
    size = {"dp": mesh.shape["dp"], "tensor": mesh.shape["tensor"]}
    return jax.shard_map(
        functools.partial(body, size),
        mesh=mesh,
        in_specs=(
            P(("dp", "tensor"), None),
            P(),
            P(None, None, "tensor"),
            P(None, "tensor"),
            P("tensor", None),
            P(),
            P(None, "tensor"),
            P(None, "tensor"),
            P("tensor", None),
            P(("dp", "tensor"), None),
        ),
        out_specs=(
            P(("dp", "tensor"), None),
            P(("dp", "tensor"), None),
            P(),
            P(None, None, "tensor"),
            P(None, "tensor"),
            P("tensor", None),
            P(),
            P(None, "tensor"),
            P(None, "tensor"),
            P("tensor", None),
        ),
        check_vma=False,
    )
```
